32 devices in a mesh: occ: 8 (over z, y), off: 4 (over x, core).
Axes of the slice: x: 2, y: 2, z: 4, core: 2. Of those that a mesh axis runs over, the one named last changes fastest.
Arguments:
- factors: bfloat16 [8, 768, 2048], P('occ'), may hold values from -0.8984375 to 0.8984375
- occ_level: int32 [8], replicated, may hold values from 0 to 255
- vir_level: int32 [768], replicated, may hold values from 0 to 255
- occupied_energy_levels: float32 [256], replicated, may hold values from -2 to -0.5
- vir_table: float32 [256], replicated, may hold values from 0.5 to 4
- virtual_coefficient_matrix: bfloat16 [768, 1024], replicated, may hold values from -0.21875 to 0.21875
Outputs:
- density_ao: float32 [8, 2048, 1024], P(None, ('occ', 'off'))
The draws below stay inside these ranges and needn't reach their ends.
Inputs may be any that keep to these rules, and one draw needn't show every extreme that they name: `occ_level`: indices into occupied_energy_levels. `vir_level`: indices into vir_table.
All inputs are finite; a program needn't handle non-finite values.
Results may differ from the reference program's by a relative error of at most 0.0032.
Values may be sent and summed in bfloat16 or wider, within the bound.
A program may use at most 64 MiB of HBM per device.

```python
import jax
import jax.numpy as jnp
from jax import lax

V = 768
NAUX = 2048
NORB = 1024
LEVELS = 256
PAIR_STEPS = 2
NOCC = 8
N_OFF = 4


def set_ends(result, rng, low, high):
    longest = result.shape.index(max(result.shape))
    spots = []
    for shift in (0, 1):
        where = [jax.random.randint(jax.random.fold_in(rng, axis), (), 0, length) for axis, length in enumerate(result.shape)]
        where[longest] = (where[longest] + shift) % result.shape[longest]
        spots.append(tuple(where))
    return result.at[spots[0]].set(low).at[spots[1]].set(high)


def level_of(own_key, extent, pieces, least, largest):
    loudness = 1.0
    for axis_at, blocks in pieces:
        steps = jax.random.uniform(jax.random.fold_in(jax.random.fold_in(own_key, 6), axis_at), (blocks,), jnp.float32, least / len(pieces), largest / len(pieces))
        loudness = loudness * jnp.repeat(jnp.exp(steps), extent[axis_at] // blocks).reshape((-1,) + (1,) * (len(extent) - 1 - axis_at))
    return loudness


def bell_draw(own_key, extent, scale, limit, cuts=(), kind=jnp.bfloat16):
    entries = scale * jax.random.normal(own_key, extent, jnp.float32)
    if cuts:
        entries = entries * level_of(own_key, extent, cuts, -0.22, 0.18)
    return jnp.clip(entries, -limit, limit).astype(kind)


def setup_inputs(seed: int = 0) -> dict:
    key_of = jax.random.split(jax.random.key(seed), 7)
    return {
        "factors": bell_draw(key_of[0], (NOCC, V, NAUX), 0.15, 0.8984375, ((0, 8),)),
        "occ_level": set_ends(jax.random.randint(key_of[1], (NOCC,), 0, LEVELS), jax.random.fold_in(key_of[1], 1), 0, LEVELS - 1).astype(jnp.int32),
        "vir_level": set_ends(jax.random.randint(key_of[2], (V,), 0, LEVELS), jax.random.fold_in(key_of[2], 1), 0, LEVELS - 1).astype(jnp.int32),
        "occupied_energy_levels": jnp.clip(jax.random.uniform(key_of[3], (LEVELS,), jnp.float32, -2.0, -0.5), -2.0, -0.5),
        "vir_table": jnp.clip(jax.random.uniform(key_of[4], (LEVELS,), jnp.float32, 0.5, 4.0), 0.5, 4.0),
        "virtual_coefficient_matrix": bell_draw(key_of[5], (V, NORB), V ** -0.5, 0.21875),
    }


def reference(factors, occ_level, vir_level, occupied_energy_levels, vir_table, virtual_coefficient_matrix):
    occ_energy = occupied_energy_levels[occ_level]
    vir_energy = vir_table[vir_level]
    offsets = N_OFF * PAIR_STEPS

    def one_orbital(orbital):
        own = lax.dynamic_index_in_dim(factors, orbital, 0, keepdims=False)
        own_energy = lax.dynamic_index_in_dim(occ_energy, orbital, 0, keepdims=False)

        def append_pair_term(offset, acc):
            pair_companion = ((orbital - offset.astype(jnp.int32)) % NOCC).astype(jnp.int32)
            other = lax.dynamic_index_in_dim(factors, pair_companion, 0, keepdims=False)
            other_energy = lax.dynamic_index_in_dim(occ_energy, pair_companion, 0, keepdims=False)
            integral = lax.dot_general(own, other, (((1,), (1,)), ((), ())), preferred_element_type=jnp.float32)
            denom = vir_energy[:, None] + vir_energy[None, :] - own_energy - other_energy
            amp = integral / denom
            pair_weight = (2.0 * amp - amp.T).astype(jnp.bfloat16)
            return acc + lax.dot_general(other, pair_weight, (((0,), (1,)), ((), ())), preferred_element_type=jnp.float32)

        gamma = lax.fori_loop(0, offsets, append_pair_term, jnp.zeros((NAUX, V), jnp.float32))
        lower_gamma_part = gamma.astype(jnp.bfloat16)
        return jnp.dot(lower_gamma_part, virtual_coefficient_matrix, preferred_element_type=jnp.float32)

    return lax.map(one_orbital, jnp.arange(NOCC, dtype=jnp.int32))
```

```python
import functools

import jax
import jax.numpy as jnp
from jax import lax
from jax.experimental import pallas as pl
from jax.experimental.pallas import tpu as pltpu
from jax.sharding import PartitionSpec as P

PAIR_STEPS = 2
PIECES = 4
MESH = pl.DeviceIdType.MESH


def passed_along(value, axis, by):
    length = lax.axis_size(axis)
    return lax.ppermute(value, axis, [(i, (i + by) % length) for i in range(length)])


def lookup(level, table):
    hits = level[:, None] == jnp.arange(table.shape[0], dtype=jnp.int32)[None, :]
    return jnp.sum(jnp.where(hits, table[None, :], jnp.float32(0.0)), axis=1)


def ring_place(occ, n):
    return jnp.where(occ % 2 == 0, occ // 2, n - 1 - occ // 2)


def ring_member(place, n):
    return jnp.where(place < n // 2, 2 * place, 2 * (n - 1 - place) + 1)


def pair_kernel(
    n,
    energy_ref,
    factors_ref,
    ev_row_ref,
    ev_col_ref,
    out_ref,
    hold,
    amp,
    weight,
    acc,
    core_out,
    core_in,
    side_out,
    side_in,
    final,
    land,
    load_sem,
    ring_send,
    ring_recv,
    side_send,
    side_recv,
    last_send,
    last_recv,
    core_sems,
    cross_sems,
    spread_send,
    spread_recv,
):
    hops = n // 2
    virt, naux = hold.shape[1], hold.shape[2]
    half = virt // 2
    piece = half // PIECES
    share = PIECES // 2
    rows = land.shape[1]
    me = lax.axis_index("occ")
    off = lax.axis_index("off")
    side, core = off // 2, off % 2
    place = ring_place(me, n)
    up = ring_member(lax.rem(place + 1, n), n)
    down = ring_member(lax.rem(place + n - 1, n), n)
    onward = jnp.where(core == 0, up, down)
    other_side = (1 - side) * 2 + core
    other_core = side * 2 + (1 - core)

    load = pltpu.make_async_copy(factors_ref.at[0], hold.at[0], load_sem)
    load.start()

    barrier = pltpu.get_barrier_semaphore()
    for step in range(1, n):
        pl.semaphore_signal(
            barrier, inc=1, device_id=(lax.rem(me + step, n), off), device_id_type=MESH
        )
    for step in range(1, 4):
        peer = lax.rem(off + step, 4)
        for node in (me, up, down):
            pl.semaphore_signal(barrier, inc=1, device_id=(node, peer), device_id_type=MESH)
    pl.semaphore_wait(barrier, n - 1 + 9)
    load.wait()

    def ring_copy(slot, m):
        where = pl.ds(pl.multiple_of(side * half + m * piece, piece), piece)
        return pltpu.make_async_remote_copy(
            src_ref=hold.at[slot, where],
            dst_ref=hold.at[slot + 1, where],
            send_sem=ring_send.at[slot, m],
            recv_sem=ring_recv.at[slot, m],
            device_id=(onward, off),
            device_id_type=MESH,
        )

    def side_copy(slot, m, from_side):
        where = pl.ds(pl.multiple_of(from_side * half + m * piece, piece), piece)
        return pltpu.make_async_remote_copy(
            src_ref=hold.at[slot, where],
            dst_ref=hold.at[slot, where],
            send_sem=side_send.at[slot - 1, m],
            recv_sem=side_recv.at[slot - 1, m],
            device_id=(me, other_side),
            device_id_type=MESH,
        )

    def last_copy(t, from_side, from_core):
        m = from_core * share + t
        where = pl.ds(pl.multiple_of(from_side * half + m * piece, piece), piece)
        return pltpu.make_async_remote_copy(
            src_ref=hold.at[hops - 1, where],
            dst_ref=hold.at[hops, where],
            send_sem=last_send.at[t],
            recv_sem=last_recv.at[from_side * PIECES + m],
            device_id=(onward, 1),
            device_id_type=MESH,
        )

    def handled(slot):
        turn = lax.rem(slot + side + core, 2) == 1
        inner = jnp.where(core == 0, slot < hops, slot > 0)
        return jnp.logical_and(turn, inner)

    def contribute(slot):
        pair_energy = energy_ref[slot]

        def integrals(h, _):
            at = pl.ds(pl.multiple_of(h * half, half), half)
            integral = lax.dot_general(
                hold[slot, at, :],
                hold[0],
                (((1,), (1,)), ((), ())),
                preferred_element_type=jnp.float32,
            )
            amp[at, :] = integral / (ev_col_ref[at, :] + ev_row_ref[...] - pair_energy)
            return 0

        lax.fori_loop(0, 2, integrals, 0)
        third = virt // 3
        for b in range(3):
            for a in range(3):
                bs, as_ = pl.ds(b * third, third), pl.ds(a * third, third)
                weight[bs, as_] = (2.0 * amp[bs, as_] - amp[as_, bs].T).astype(jnp.bfloat16)

        part = naux // 4

        def gammas(p, _):
            at = pl.ds(pl.multiple_of(p * part, part), part)
            acc[at, :] += lax.dot_general(
                hold[slot, :, at],
                weight[...],
                (((0,), (0,)), ((), ())),
                preferred_element_type=jnp.float32,
            )
            return 0

        lax.fori_loop(0, 4, gammas, 0)

    for m in range(PIECES):
        ring_copy(0, m).start()

    def clear(p, _):
        at = pl.ds(pl.multiple_of(p * 4 * rows, 4 * rows), 4 * rows)
        acc[at, :] = jnp.zeros((4 * rows, virt), jnp.float32)
        return 0

    lax.fori_loop(0, n, clear, 0)

    def stage(slot, _):
        middle = jnp.logical_and(slot >= 1, slot < hops)

        @pl.when(middle)
        def _():
            for m in range(PIECES):
                ring_copy(slot - 1, m).wait_recv()

                @pl.when(slot < hops - 1)
                def _():
                    ring_copy(slot, m).start()

                @pl.when(jnp.logical_not(handled(slot)))
                def _():
                    side_copy(slot, m, side).start()

        @pl.when(slot == hops - 1)
        def _():
            for t in range(share):
                last_copy(t, side, core).start()

        @pl.when(handled(slot))
        def _():
            @pl.when(middle)
            def _():
                for m in range(PIECES):
                    side_copy(slot, m, 1 - side).wait_recv()

            @pl.when(slot == hops)
            def _():
                for s in range(2):
                    for c in range(2):
                        for t in range(share):
                            last_copy(t, s, c).wait_recv()

            contribute(slot)

        return 0

    lax.fori_loop(0, hops + 1, stage, 0)

    def core_copy(k):
        return pltpu.make_async_remote_copy(
            src_ref=core_out.at[k],
            dst_ref=core_in.at[k],
            send_sem=core_sems.at[0, k],
            recv_sem=core_sems.at[1, k],
            device_id=(me, other_core),
            device_id_type=MESH,
        )

    def cross_copy(k):
        return pltpu.make_async_remote_copy(
            src_ref=side_out.at[k],
            dst_ref=side_in.at[k],
            send_sem=cross_sems.at[0, k],
            recv_sem=cross_sems.at[1, k],
            device_id=(me, other_side),
            device_id_type=MESH,
        )

    def spread_copy(k, source):
        return pltpu.make_async_remote_copy(
            src_ref=final.at[k],
            dst_ref=land.at[source],
            send_sem=spread_send.at[k],
            recv_sem=spread_recv.at[source],
            device_id=(k, off),
            device_id_type=MESH,
        )

    def chunk(k, s, c):
        return pl.ds(pl.multiple_of(((k * 2 + s) * 2 + c) * rows, rows), rows)

    def to_core(t, _):
        k = lax.rem(me + 1 + t, n)
        for s in range(2):
            core_out[k, s] = acc[chunk(k, s, 1 - core), :].astype(jnp.bfloat16)
        core_copy(k).start()
        return 0

    lax.fori_loop(0, n, to_core, 0)

    def to_side(t, _):
        k = lax.rem(me + 1 + t, n)
        core_copy(k).wait_recv()
        theirs = acc[chunk(k, 1 - side, core), :] + core_in[k, 1 - side].astype(jnp.float32)
        side_out[k] = theirs.astype(jnp.bfloat16)
        cross_copy(k).start()
        return 0

    lax.fori_loop(0, n, to_side, 0)

    def to_owner(t, _):
        k = lax.rem(me + 1 + t, n)
        cross_copy(k).wait_recv()
        mine = acc[chunk(k, side, core), :] + core_in[k, side].astype(jnp.float32)
        mine = (mine + side_in[k].astype(jnp.float32)).astype(jnp.bfloat16)

        @pl.when(t < n - 1)
        def _():
            final[k] = mine
            spread_copy(k, me).start()

        @pl.when(t == n - 1)
        def _():
            out_ref[me] = mine

        return 0

    lax.fori_loop(0, n, to_owner, 0)

    def settle(t, _):
        k = lax.rem(me + 1 + t, n)
        spread_copy(k, k).wait_recv()
        out_ref[k] = land[k]
        return 0

    lax.fori_loop(0, n - 1, settle, 0)

    for slot in range(hops - 1):
        for m in range(PIECES):
            ring_copy(slot, m).wait_send()

    def sent(slot, _):
        @pl.when(jnp.logical_not(handled(slot)))
        def _():
            for m in range(PIECES):
                side_copy(slot, m, side).wait_send()

        return 0

    lax.fori_loop(1, hops, sent, 0)
    for t in range(share):
        last_copy(t, side, core).wait_send()

    def closed(t, _):
        k = lax.rem(me + 1 + t, n)
        core_copy(k).wait_send()
        cross_copy(k).wait_send()

        @pl.when(t < n - 1)
        def _():
            spread_copy(k, me).wait_send()

        return 0

    lax.fori_loop(0, n, closed, 0)


def ring_body(
    factors, occ_level, vir_level, occupied_energy_levels, vir_table, virtual_coefficient_matrix
):
    n = lax.axis_size("occ")
    hops = n // 2
    off = lax.axis_index("off")
    me = lax.axis_index("occ")
    virt, naux = factors.shape[1], factors.shape[2]
    rows = naux // (n * lax.axis_size("off"))
    ev = lookup(vir_level, vir_table)
    eo = lookup(occ_level, occupied_energy_levels)
    turn = jnp.where(off % 2 == 0, -1, 1)
    partners = ring_member((ring_place(me, n) + turn * jnp.arange(hops + 1)) % n, n)
    own_energy = lax.dynamic_index_in_dim(eo, me, 0, keepdims=False)
    hit = partners[:, None] == jnp.arange(n)[None, :]
    energy = own_energy + jnp.sum(jnp.where(hit, eo[None, :], jnp.float32(0.0)), axis=1)
    vmem = pl.BlockSpec(memory_space=pltpu.VMEM)
    dma = pltpu.SemaphoreType.DMA
    gamma_low = pl.pallas_call(
        functools.partial(pair_kernel, n),
        out_shape=jax.ShapeDtypeStruct((n, rows, virt), jnp.bfloat16),
        in_specs=[
            pl.BlockSpec(memory_space=pltpu.SMEM),
            pl.BlockSpec(memory_space=pl.ANY),
            vmem,
            vmem,
        ],
        out_specs=vmem,
        scratch_shapes=[
            pltpu.VMEM((hops + 1, virt, naux), jnp.bfloat16),
            pltpu.VMEM((virt, virt), jnp.float32),
            pltpu.VMEM((virt, virt), jnp.bfloat16),
            pltpu.VMEM((naux, virt), jnp.float32),
            pltpu.VMEM((n, 2, rows, virt), jnp.bfloat16),
            pltpu.VMEM((n, 2, rows, virt), jnp.bfloat16),
            pltpu.VMEM((n, rows, virt), jnp.bfloat16),
            pltpu.VMEM((n, rows, virt), jnp.bfloat16),
            pltpu.VMEM((n, rows, virt), jnp.bfloat16),
            pltpu.VMEM((n, rows, virt), jnp.bfloat16),
            dma,
            dma((hops - 1, PIECES)),
            dma((hops - 1, PIECES)),
            dma((hops - 1, PIECES)),
            dma((hops - 1, PIECES)),
            dma((PIECES // 2,)),
            dma((2 * PIECES,)),
            dma((2, n)),
            dma((2, n)),
            dma((n,)),
            dma((n,)),
        ],
        compiler_params=pltpu.CompilerParams(
            collective_id=0, has_side_effects=True, vmem_limit_bytes=56 * 1024 * 1024
        ),
        cost_estimate=pl.CostEstimate(
            flops=8 * virt * virt * naux, bytes_accessed=2 * virt * naux, transcendentals=0
        ),
    )(energy, factors, ev[None, :], ev[:, None])
    return jnp.einsum(
        "sbd,dw->sbw",
        gamma_low,
        virtual_coefficient_matrix,
        preferred_element_type=jnp.float32,
    )


def general_body(
    factors, occ_level, vir_level, occupied_energy_levels, vir_table, virtual_coefficient_matrix
):
    off_count = lax.axis_size("off")
    off_index = lax.axis_index("off")
    occ_count = lax.axis_size("occ")
    occ_index = lax.axis_index("occ")
    vir_energy = lookup(vir_level, vir_table)
    occ_energy = lookup(occ_level, occupied_energy_levels)
    own_energy = lax.dynamic_index_in_dim(occ_energy, occ_index, 0, keepdims=False)
    own = factors[0]
    carried = factors
    for bit_pos in range(off_count.bit_length() - 1):
        moved = passed_along(carried, "occ", 1 << bit_pos)
        carried = jnp.where(off_index >> bit_pos & 1 == 1, moved, carried)
    gamma = jnp.zeros((own.shape[1], own.shape[0]), jnp.float32)
    for step_index in range(PAIR_STEPS):
        offset = off_index + off_count * step_index
        pair_companion = (occ_index - offset) % occ_count
        other_energy = lax.dynamic_index_in_dim(occ_energy, pair_companion, 0, keepdims=False)
        other = carried[0]
        if step_index < PAIR_STEPS - 1:
            carried = passed_along(carried, "occ", off_count)
        integral = lax.dot_general(
            own, other, (((1,), (1,)), ((), ())), preferred_element_type=jnp.float32
        )
        denom = vir_energy[:, None] + vir_energy[None, :] - own_energy - other_energy
        amp = integral / denom
        pair_weight = (2.0 * amp - amp.T).astype(jnp.bfloat16)
        gamma = gamma + lax.dot_general(
            other, pair_weight, (((0,), (1,)), ((), ())), preferred_element_type=jnp.float32
        )
    naux_rows = gamma.shape[0]
    per_device = naux_rows // (occ_count * off_count)
    blocks = gamma.reshape(occ_count, off_count, per_device, gamma.shape[1])
    total = lax.psum(blocks, "off")
    mine = lax.dynamic_slice_in_dim(total, off_index, 1, 1)
    lower_gamma_part = mine.reshape(occ_count, per_device, gamma.shape[1]).astype(jnp.bfloat16)
    finished_flag = jnp.einsum(
        "sbd,dw->sbw",
        lower_gamma_part,
        virtual_coefficient_matrix,
        preferred_element_type=jnp.float32,
    )
    moved_back = lax.all_to_all(finished_flag[None], "occ", split_axis=1, concat_axis=0, tiled=True)
    return moved_back.reshape(moved_back.shape[0], per_device, virtual_coefficient_matrix.shape[1])


def solution(mesh):
    in_specs = (P("occ", None, None), P(), P(), P(), P(), P())
    out_specs = P(None, ("occ", "off"), None)
    every_pair = mesh.shape["occ"] == mesh.shape["off"] * PAIR_STEPS
    ring = every_pair and mesh.shape["off"] == 4
    body = ring_body if ring else general_body
    return jax.shard_map(body, mesh=mesh, in_specs=in_specs, out_specs=out_specs, check_vma=False)
```

```python
import functools

import jax
import jax.numpy as jnp
from jax import lax
from jax.experimental import pallas as pl
from jax.experimental.pallas import tpu as pltpu
from jax.sharding import PartitionSpec as P

PAIR_STEPS = 2
PIECES = 4
MESH = pl.DeviceIdType.MESH


def passed_along(value, axis, by):
    length = lax.axis_size(axis)
    return lax.ppermute(value, axis, [(i, (i + by) % length) for i in range(length)])


def lookup(level, table):
    hits = level[:, None] == jnp.arange(table.shape[0], dtype=jnp.int32)[None, :]
    return jnp.sum(jnp.where(hits, table[None, :], jnp.float32(0.0)), axis=1)


def ring_place(occ, n):
    return jnp.where(occ % 2 == 0, occ // 2, n - 1 - occ // 2)


def ring_member(place, n):
    return jnp.where(place < n // 2, 2 * place, 2 * (n - 1 - place) + 1)


def pair_kernel(
    n,
    occ_level_ref,
    occ_table_ref,
    factors_ref,
    vir_level_ref,
    vir_table_ref,
    out_ref,
    ev_row_ref,
    ev_col_ref,
    hold,
    amp,
    weight,
    acc,
    core_out,
    core_in,
    side_out,
    side_in,
    final,
    land,
    load_sem,
    ring_send,
    ring_recv,
    side_send,
    side_recv,
    last_send,
    last_recv,
    pass_send,
    core_sems,
    cross_sems,
    spread_send,
    spread_recv,
):
    hops = n // 2
    virt, naux = hold.shape[1], hold.shape[2]
    half = virt // 2
    piece = half // PIECES
    share = PIECES // 2
    rows = land.shape[1]
    me = lax.axis_index("occ")
    off = lax.axis_index("off")
    side, core = off // 2, off % 2
    place = ring_place(me, n)
    up = ring_member(lax.rem(place + 1, n), n)
    down = ring_member(lax.rem(place + n - 1, n), n)
    onward = jnp.where(core == 0, up, down)
    other_side = (1 - side) * 2 + core
    other_core = side * 2 + (1 - core)

    load = pltpu.make_async_copy(factors_ref.at[0], hold.at[0], load_sem)
    load.start()

    barrier = pltpu.get_barrier_semaphore()
    for step in range(1, n):
        pl.semaphore_signal(
            barrier, inc=1, device_id=(lax.rem(me + step, n), off), device_id_type=MESH
        )
    for step in range(1, 4):
        peer = lax.rem(off + step, 4)
        for node in (me, up, down):
            pl.semaphore_signal(barrier, inc=1, device_id=(node, peer), device_id_type=MESH)
    pl.semaphore_wait(barrier, n - 1 + 9)
    load.wait()

    def ring_copy(slot, m):
        where = pl.ds(pl.multiple_of(side * half + m * piece, piece), piece)
        return pltpu.make_async_remote_copy(
            src_ref=hold.at[slot, where],
            dst_ref=hold.at[slot + 1, where],
            send_sem=ring_send.at[slot, m],
            recv_sem=ring_recv.at[slot, m],
            device_id=(onward, off),
            device_id_type=MESH,
        )

    def side_copy(slot, m, from_side):
        where = pl.ds(pl.multiple_of(from_side * half + m * piece, piece), piece)
        return pltpu.make_async_remote_copy(
            src_ref=hold.at[slot, where],
            dst_ref=hold.at[slot, where],
            send_sem=side_send.at[slot - 1, m],
            recv_sem=side_recv.at[slot - 1, m],
            device_id=(me, other_side),
            device_id_type=MESH,
        )

    def last_copy(t, from_side, from_core):
        m = from_core * share + t
        where = pl.ds(pl.multiple_of(from_side * half + m * piece, piece), piece)
        return pltpu.make_async_remote_copy(
            src_ref=hold.at[hops - 1, where],
            dst_ref=hold.at[hops, where],
            send_sem=last_send.at[t],
            recv_sem=last_recv.at[from_side * PIECES + m],
            device_id=(onward, jnp.where(side == 0, 1, off)),
            device_id_type=MESH,
        )

    def pass_copy(t):
        m = core * share + t
        where = pl.ds(pl.multiple_of(side * half + m * piece, piece), piece)
        return pltpu.make_async_remote_copy(
            src_ref=hold.at[hops, where],
            dst_ref=hold.at[hops, where],
            send_sem=pass_send.at[t],
            recv_sem=last_recv.at[side * PIECES + m],
            device_id=(me, 1),
            device_id_type=MESH,
        )

    def handled(slot):
        turn = lax.rem(slot + side + core, 2) == 1
        inner = jnp.where(core == 0, slot < hops, slot > 0)
        return jnp.logical_and(turn, inner)

    def occ_energy(orbital):
        return occ_table_ref[occ_level_ref[orbital]]

    def integrals(slot, h):
        turn = jnp.where(core == 0, n - slot, slot)
        partner = ring_member(lax.rem(place + turn, n), n)
        pair_energy = occ_energy(me) + occ_energy(partner)
        at = pl.ds(pl.multiple_of(h * half, half), half)
        integral = lax.dot_general(
            hold[slot, at, :],
            hold[0],
            (((1,), (1,)), ((), ())),
            preferred_element_type=jnp.float32,
        )
        amp[at, :] = integral / (ev_col_ref[at, :] + ev_row_ref[...] - pair_energy)

    def weights():
        third = virt // 3
        for b in range(3):
            for a in range(3):
                bs, as_ = pl.ds(b * third, third), pl.ds(a * third, third)
                weight[bs, as_] = (2.0 * amp[bs, as_] - amp[as_, bs].T).astype(jnp.bfloat16)

    def gammas(slot, p, part):
        at = pl.ds(pl.multiple_of(p * part, part), part)
        acc[at, :] += lax.dot_general(
            hold[slot, :, at],
            weight[...],
            (((0,), (0,)), ((), ())),
            preferred_element_type=jnp.float32,
        )

    def work(slot, m):
        if m == 0:
            integrals(slot, side)
        elif m == 1:

            @pl.when(slot > 0)
            def _():
                for q in range(PIECES):
                    side_copy(slot, q, 1 - side).wait_recv()

            integrals(slot, 1 - side)
        else:
            if m == 2:
                weights()

            def two(p, _):
                gammas(slot, 2 * (m - 2) + p, naux // 4)
                return 0

            lax.fori_loop(0, 2, two, 0)

    for m in range(PIECES):
        ring_copy(0, m).start()

    def clear(p, _):
        at = pl.ds(pl.multiple_of(p * 4 * rows, 4 * rows), 4 * rows)
        acc[at, :] = jnp.zeros((4 * rows, virt), jnp.float32)
        return 0

    lax.fori_loop(0, n, clear, 0)

    levels = vir_table_ref.shape[1]
    same = lax.broadcasted_iota(jnp.int32, (levels, levels), 0) == lax.broadcasted_iota(
        jnp.int32, (levels, levels), 1
    )
    table = jnp.sum(jnp.where(same, vir_table_ref[...], 0.0), axis=1, keepdims=True)
    hits = lax.broadcasted_iota(jnp.int32, (levels, virt), 0) == vir_level_ref[...]
    row = jnp.sum(jnp.where(hits, table, 0.0), axis=0, keepdims=True)
    ev_row_ref[...] = row
    same = lax.broadcasted_iota(jnp.int32, (virt, virt), 0) == lax.broadcasted_iota(
        jnp.int32, (virt, virt), 1
    )
    ev_col_ref[...] = jnp.sum(jnp.where(same, row, 0.0), axis=1, keepdims=True)

    def stage(slot, _):
        for m in range(PIECES):

            @pl.when(slot < hops)
            def _():
                ring_copy(slot - 1, m).wait_recv()

                @pl.when(slot < hops - 1)
                def _():
                    ring_copy(slot, m).start()

                @pl.when(jnp.logical_not(handled(slot)))
                def _():
                    side_copy(slot, m, side).start()

            if m < share:

                @pl.when(jnp.logical_and(slot == hops, side == 1))
                def _():
                    last_copy(m, side, core).wait_recv()
                    pass_copy(m).start()

            if m == PIECES - 1:

                @pl.when(slot == hops - 1)
                def _():
                    for t in range(share):
                        last_copy(t, side, core).start()

            @pl.when(handled(slot - 1))
            def _():
                work(slot - 1, m)

        return 0

    lax.fori_loop(1, hops + 1, stage, 0)

    late = handled(hops)

    @pl.when(late)
    def _():
        for s in range(2):
            for c in range(2):
                for t in range(share):
                    last_copy(t, s, c).wait_recv()
            integrals(hops, s)
        weights()

    def core_copy(k):
        return pltpu.make_async_remote_copy(
            src_ref=core_out.at[k],
            dst_ref=core_in.at[k],
            send_sem=core_sems.at[0, k],
            recv_sem=core_sems.at[1, k],
            device_id=(me, other_core),
            device_id_type=MESH,
        )

    def cross_copy(k):
        return pltpu.make_async_remote_copy(
            src_ref=side_out.at[k],
            dst_ref=side_in.at[k],
            send_sem=cross_sems.at[0, k],
            recv_sem=cross_sems.at[1, k],
            device_id=(me, other_side),
            device_id_type=MESH,
        )

    def spread_copy(k, source):
        return pltpu.make_async_remote_copy(
            src_ref=final.at[k],
            dst_ref=land.at[source],
            send_sem=spread_send.at[k],
            recv_sem=spread_recv.at[source],
            device_id=(k, off),
            device_id_type=MESH,
        )

    def chunk(k, s, c):
        return pl.ds(pl.multiple_of(((k * 2 + s) * 2 + c) * rows, rows), rows)

    def target(t):
        flip = jnp.where(t < n // 2, n // 2 + t, n - 1 - t)
        k = 0
        for bit in range(n.bit_length() - 1):
            k = k + ((me // 2**bit + flip // 2**bit) % 2) * 2**bit
        return k

    def to_side(t, _):
        k = target(t)

        @pl.when(late)
        def _():
            gammas(hops, k, 4 * rows)

        for s in range(2):
            core_out[k, s] = acc[chunk(k, s, 1 - core), :].astype(jnp.bfloat16)
        core_copy(k).start()
        core_copy(k).wait_recv()
        theirs = acc[chunk(k, 1 - side, core), :] + core_in[k, 1 - side].astype(jnp.float32)
        side_out[k] = theirs.astype(jnp.bfloat16)
        cross_copy(k).start()
        return 0

    lax.fori_loop(0, n, to_side, 0)

    def to_owner(t, _):
        k = target(t)
        cross_copy(k).wait_recv()
        mine = acc[chunk(k, side, core), :] + core_in[k, side].astype(jnp.float32)
        mine = (mine + side_in[k].astype(jnp.float32)).astype(jnp.bfloat16)

        @pl.when(t < n - 1)
        def _():
            final[k] = mine
            spread_copy(k, me).start()

        @pl.when(t == n - 1)
        def _():
            out_ref[me] = mine

        return 0

    lax.fori_loop(0, n, to_owner, 0)

    def settle(t, _):
        k = target(t)
        spread_copy(k, k).wait_recv()
        out_ref[k] = land[k]
        return 0

    lax.fori_loop(0, n - 1, settle, 0)

    for slot in range(hops - 1):
        for m in range(PIECES):
            ring_copy(slot, m).wait_send()

    def sent(slot, _):
        @pl.when(jnp.logical_not(handled(slot)))
        def _():
            for m in range(PIECES):
                side_copy(slot, m, side).wait_send()

        return 0

    lax.fori_loop(1, hops, sent, 0)
    for t in range(share):
        last_copy(t, side, core).wait_send()

        @pl.when(side == 1)
        def _():
            pass_copy(t).wait_send()


    def closed(t, _):
        k = target(t)
        core_copy(k).wait_send()
        cross_copy(k).wait_send()

        @pl.when(t < n - 1)
        def _():
            spread_copy(k, me).wait_send()

        return 0

    lax.fori_loop(0, n, closed, 0)


def ring_body(
    factors, occ_level, vir_level, occupied_energy_levels, vir_table, virtual_coefficient_matrix
):
    n = lax.axis_size("occ")
    hops = n // 2
    virt, naux = factors.shape[1], factors.shape[2]
    rows = naux // (n * lax.axis_size("off"))
    smem = pl.BlockSpec(memory_space=pltpu.SMEM)
    vmem = pl.BlockSpec(memory_space=pltpu.VMEM)
    dma = pltpu.SemaphoreType.DMA
    gamma_low = pl.pallas_call(
        functools.partial(pair_kernel, n),
        out_shape=jax.ShapeDtypeStruct((n, rows, virt), jnp.bfloat16),
        in_specs=[
            smem,
            smem,
            pl.BlockSpec(memory_space=pl.ANY),
            vmem,
            vmem,
        ],
        out_specs=vmem,
        scratch_shapes=[
            pltpu.VMEM((1, virt), jnp.float32),
            pltpu.VMEM((virt, 1), jnp.float32),
            pltpu.VMEM((hops + 1, virt, naux), jnp.bfloat16),
            pltpu.VMEM((virt, virt), jnp.float32),
            pltpu.VMEM((virt, virt), jnp.bfloat16),
            pltpu.VMEM((naux, virt), jnp.float32),
            pltpu.VMEM((n, 2, rows, virt), jnp.bfloat16),
            pltpu.VMEM((n, 2, rows, virt), jnp.bfloat16),
            pltpu.VMEM((n, rows, virt), jnp.bfloat16),
            pltpu.VMEM((n, rows, virt), jnp.bfloat16),
            pltpu.VMEM((n, rows, virt), jnp.bfloat16),
            pltpu.VMEM((n, rows, virt), jnp.bfloat16),
            dma,
            dma((hops - 1, PIECES)),
            dma((hops - 1, PIECES)),
            dma((hops - 1, PIECES)),
            dma((hops - 1, PIECES)),
            dma((PIECES // 2,)),
            dma((2 * PIECES,)),
            dma((PIECES // 2,)),
            dma((2, n)),
            dma((2, n)),
            dma((n,)),
            dma((n,)),
        ],
        compiler_params=pltpu.CompilerParams(
            collective_id=0, has_side_effects=True, vmem_limit_bytes=56 * 1024 * 1024
        ),
        cost_estimate=pl.CostEstimate(
            flops=8 * virt * virt * naux, bytes_accessed=2 * virt * naux, transcendentals=0
        ),
    )(occ_level, occupied_energy_levels, factors, vir_level[None, :], vir_table[None, :])
    return jnp.einsum(
        "sbd,dw->sbw",
        gamma_low,
        virtual_coefficient_matrix,
        preferred_element_type=jnp.float32,
    )


def general_body(
    factors, occ_level, vir_level, occupied_energy_levels, vir_table, virtual_coefficient_matrix
):
    off_count = lax.axis_size("off")
    off_index = lax.axis_index("off")
    occ_count = lax.axis_size("occ")
    occ_index = lax.axis_index("occ")
    vir_energy = lookup(vir_level, vir_table)
    occ_energy = lookup(occ_level, occupied_energy_levels)
    own_energy = lax.dynamic_index_in_dim(occ_energy, occ_index, 0, keepdims=False)
    own = factors[0]
    carried = factors
    for bit_pos in range(off_count.bit_length() - 1):
        moved = passed_along(carried, "occ", 1 << bit_pos)
        carried = jnp.where(off_index >> bit_pos & 1 == 1, moved, carried)
    gamma = jnp.zeros((own.shape[1], own.shape[0]), jnp.float32)
    for step_index in range(PAIR_STEPS):
        offset = off_index + off_count * step_index
        pair_companion = (occ_index - offset) % occ_count
        other_energy = lax.dynamic_index_in_dim(occ_energy, pair_companion, 0, keepdims=False)
        other = carried[0]
        if step_index < PAIR_STEPS - 1:
            carried = passed_along(carried, "occ", off_count)
        integral = lax.dot_general(
            own, other, (((1,), (1,)), ((), ())), preferred_element_type=jnp.float32
        )
        denom = vir_energy[:, None] + vir_energy[None, :] - own_energy - other_energy
        amp = integral / denom
        pair_weight = (2.0 * amp - amp.T).astype(jnp.bfloat16)
        gamma = gamma + lax.dot_general(
            other, pair_weight, (((0,), (1,)), ((), ())), preferred_element_type=jnp.float32
        )
    naux_rows = gamma.shape[0]
    per_device = naux_rows // (occ_count * off_count)
    blocks = gamma.reshape(occ_count, off_count, per_device, gamma.shape[1])
    total = lax.psum(blocks, "off")
    mine = lax.dynamic_slice_in_dim(total, off_index, 1, 1)
    lower_gamma_part = mine.reshape(occ_count, per_device, gamma.shape[1]).astype(jnp.bfloat16)
    finished_flag = jnp.einsum(
        "sbd,dw->sbw",
        lower_gamma_part,
        virtual_coefficient_matrix,
        preferred_element_type=jnp.float32,
    )
    moved_back = lax.all_to_all(finished_flag[None], "occ", split_axis=1, concat_axis=0, tiled=True)
    return moved_back.reshape(moved_back.shape[0], per_device, virtual_coefficient_matrix.shape[1])


def solution(mesh):
    in_specs = (P("occ", None, None), P(), P(), P(), P(), P())
    out_specs = P(None, ("occ", "off"), None)
    every_pair = mesh.shape["occ"] == mesh.shape["off"] * PAIR_STEPS
    ring = every_pair and mesh.shape["off"] == 4
    body = ring_body if ring else general_body
    return jax.shard_map(body, mesh=mesh, in_specs=in_specs, out_specs=out_specs, check_vma=False)
```

```python
import functools

import jax
import jax.numpy as jnp
from jax import lax
from jax.experimental import pallas as pl
from jax.experimental.pallas import tpu as pltpu
from jax.sharding import PartitionSpec as P

PAIR_STEPS = 2
PIECES = 4
MESH = pl.DeviceIdType.MESH


def passed_along(value, axis, by):
    length = lax.axis_size(axis)
    return lax.ppermute(value, axis, [(i, (i + by) % length) for i in range(length)])


def lookup(level, table):
    hits = level[:, None] == jnp.arange(table.shape[0], dtype=jnp.int32)[None, :]
    return jnp.sum(jnp.where(hits, table[None, :], jnp.float32(0.0)), axis=1)


def ring_place(occ, n):
    return jnp.where(occ % 2 == 0, occ // 2, n - 1 - occ // 2)


def ring_member(place, n):
    return jnp.where(place < n // 2, 2 * place, 2 * (n - 1 - place) + 1)


def pair_kernel(
    n,
    occ_level_ref,
    occ_table_ref,
    factors_ref,
    vir_level_ref,
    vir_table_ref,
    out_ref,
    ev_row_ref,
    ev_col_ref,
    hold,
    amp,
    weight,
    acc,
    core_out,
    core_in,
    side_out,
    side_in,
    final,
    land,
    load_sem,
    ring_send,
    ring_recv,
    side_send,
    side_recv,
    last_send,
    last_recv,
    core_sems,
    cross_sems,
    spread_send,
    spread_recv,
):
    hops = n // 2
    virt, naux = hold.shape[1], hold.shape[2]
    half = virt // 2
    piece = half // PIECES
    rows = land.shape[1]
    me = lax.axis_index("occ")
    off = lax.axis_index("off")
    side, core = off // 2, off % 2
    place = ring_place(me, n)
    up = ring_member(lax.rem(place + 1, n), n)
    down = ring_member(lax.rem(place + n - 1, n), n)
    onward = jnp.where(core == 0, up, down)
    other_side = (1 - side) * 2 + core
    other_core = side * 2 + (1 - core)

    load = pltpu.make_async_copy(factors_ref.at[0], hold.at[0], load_sem)
    load.start()

    barrier = pltpu.get_barrier_semaphore()
    for step in range(1, n):
        pl.semaphore_signal(
            barrier, inc=1, device_id=(lax.rem(me + step, n), off), device_id_type=MESH
        )
    for step in range(1, 4):
        peer = lax.rem(off + step, 4)
        for node in (me, up, down):
            pl.semaphore_signal(barrier, inc=1, device_id=(node, peer), device_id_type=MESH)
    pl.semaphore_wait(barrier, n - 1 + 9)
    load.wait()

    def ring_copy(slot, m):
        where = pl.ds(pl.multiple_of(side * half + m * piece, piece), piece)
        return pltpu.make_async_remote_copy(
            src_ref=hold.at[slot, where],
            dst_ref=hold.at[slot + 1, where],
            send_sem=ring_send.at[slot, m],
            recv_sem=ring_recv.at[slot, m],
            device_id=(onward, off),
            device_id_type=MESH,
        )

    def side_copy(slot, m, from_side):
        where = pl.ds(pl.multiple_of(from_side * half + m * piece, piece), piece)
        return pltpu.make_async_remote_copy(
            src_ref=hold.at[slot, where],
            dst_ref=hold.at[slot, where],
            send_sem=side_send.at[slot - 1, m],
            recv_sem=side_recv.at[slot - 1, m],
            device_id=(me, other_side),
            device_id_type=MESH,
        )

    def last_copy(m, part):
        where = pl.ds(pl.multiple_of(part * half + m * piece, piece), piece)
        return pltpu.make_async_remote_copy(
            src_ref=hold.at[hops - 1, where],
            dst_ref=hold.at[hops, where],
            send_sem=last_send.at[m],
            recv_sem=last_recv.at[part * PIECES + m],
            device_id=(onward, side * 2 + (1 - side)),
            device_id_type=MESH,
        )

    def handled(slot):
        turn = lax.rem(slot + side + core, 2) == 1
        return jnp.logical_and(turn, jnp.logical_or(core == 0, slot > 0))

    def occ_energy(orbital):
        return occ_table_ref[occ_level_ref[orbital]]

    def integrals(slot, h):
        turn = jnp.where(core == 0, n - slot, slot)
        partner = ring_member(lax.rem(place + turn, n), n)
        pair_energy = occ_energy(me) + occ_energy(partner)
        at = pl.ds(pl.multiple_of(h * half, half), half)
        integral = lax.dot_general(
            hold[slot, at, :],
            hold[0],
            (((1,), (1,)), ((), ())),
            preferred_element_type=jnp.float32,
        )
        amp[at, :] = integral / (ev_col_ref[at, :] + ev_row_ref[...] - pair_energy)

    def weights():
        third = virt // 3
        for b in range(3):
            for a in range(3):
                bs, as_ = pl.ds(b * third, third), pl.ds(a * third, third)
                weight[bs, as_] = (2.0 * amp[bs, as_] - amp[as_, bs].T).astype(jnp.bfloat16)

    def gammas(slot, p, part):
        at = pl.ds(pl.multiple_of(p * part, part), part)
        acc[at, :] += lax.dot_general(
            hold[slot, :, at],
            weight[...],
            (((0,), (0,)), ((), ())),
            preferred_element_type=jnp.float32,
        )

    def work(slot, m):
        if m == 0:
            integrals(slot, side)
        elif m == 1:

            @pl.when(jnp.logical_and(slot > 0, slot < hops - 1))
            def _():
                for q in range(PIECES):
                    side_copy(slot, q, 1 - side).wait_recv()

            integrals(slot, 1 - side)
        else:
            if m == 2:
                weights()

            def two(p, _):
                gammas(slot, 2 * (m - 2) + p, naux // 4)
                return 0

            lax.fori_loop(0, 2, two, 0)

    for m in range(PIECES):
        ring_copy(0, m).start()

    def clear(p, _):
        at = pl.ds(pl.multiple_of(p * 4 * rows, 4 * rows), 4 * rows)
        acc[at, :] = jnp.zeros((4 * rows, virt), jnp.float32)
        return 0

    lax.fori_loop(0, n, clear, 0)

    levels = vir_table_ref.shape[1]
    same = lax.broadcasted_iota(jnp.int32, (levels, levels), 0) == lax.broadcasted_iota(
        jnp.int32, (levels, levels), 1
    )
    table = jnp.sum(jnp.where(same, vir_table_ref[...], 0.0), axis=1, keepdims=True)
    hits = lax.broadcasted_iota(jnp.int32, (levels, virt), 0) == vir_level_ref[...]
    row = jnp.sum(jnp.where(hits, table, 0.0), axis=0, keepdims=True)
    ev_row_ref[...] = row
    same = lax.broadcasted_iota(jnp.int32, (virt, virt), 0) == lax.broadcasted_iota(
        jnp.int32, (virt, virt), 1
    )
    ev_col_ref[...] = jnp.sum(jnp.where(same, row, 0.0), axis=1, keepdims=True)

    def stage(slot, _):
        for m in range(PIECES):

            @pl.when(slot < hops)
            def _():
                ring_copy(slot - 1, m).wait_recv()

                @pl.when(slot < hops - 1)
                def _():
                    ring_copy(slot, m).start()

                @pl.when(jnp.logical_not(handled(slot)))
                def _():
                    side_copy(slot, m, side).start()

            @pl.when(jnp.logical_and(slot == hops - 1, jnp.logical_not(handled(slot))))
            def _():
                last_copy(m, 1 - core).start()

            if m == 0:

                @pl.when(jnp.logical_and(slot == hops, handled(hops - 1)))
                def _():
                    for q in range(PIECES):
                        side_copy(hops - 1, q, 1 - side).wait_recv()
                        last_copy(q, 1 - core).start()

            @pl.when(handled(slot - 1))
            def _():
                work(slot - 1, m)

        return 0

    lax.fori_loop(1, hops + 1, stage, 0)

    late = handled(hops)

    def core_copy(k, s, when):
        return pltpu.make_async_remote_copy(
            src_ref=core_out.at[k, s],
            dst_ref=core_in.at[k, s],
            send_sem=core_sems.at[2 * when, k],
            recv_sem=core_sems.at[2 * when + 1, k],
            device_id=(me, other_core),
            device_id_type=MESH,
        )

    def cross_copy(k):
        return pltpu.make_async_remote_copy(
            src_ref=side_out.at[k],
            dst_ref=side_in.at[k],
            send_sem=cross_sems.at[0, k],
            recv_sem=cross_sems.at[1, k],
            device_id=(me, other_side),
            device_id_type=MESH,
        )

    def spread_copy(k, source):
        return pltpu.make_async_remote_copy(
            src_ref=final.at[k],
            dst_ref=land.at[source],
            send_sem=spread_send.at[k],
            recv_sem=spread_recv.at[source],
            device_id=(k, off),
            device_id_type=MESH,
        )

    def chunk(k, s, c):
        return pl.ds(pl.multiple_of(((k * 2 + s) * 2 + c) * rows, rows), rows)

    def target(t):
        flip = jnp.where(t < n // 2, n // 2 + t, n - 1 - t)
        k = 0
        for bit in range(n.bit_length() - 1):
            k = k + ((me // 2**bit + flip // 2**bit) % 2) * 2**bit
        return k

    def to_core(t, _):
        k = target(t)
        core_out[k, 1 - side] = acc[chunk(k, 1 - side, 1 - core), :].astype(jnp.bfloat16)
        core_copy(k, 1 - side, 0).start()
        return 0

    lax.fori_loop(0, n, to_core, 0)

    def to_side(t, _):
        k = target(t)
        core_copy(k, 1 - side, 0).wait_recv()
        theirs = acc[chunk(k, 1 - side, core), :] + core_in[k, 1 - side].astype(jnp.float32)
        side_out[k] = theirs.astype(jnp.bfloat16)
        cross_copy(k).start()
        return 0

    lax.fori_loop(0, n, to_side, 0)

    @pl.when(late)
    def _():
        for part in range(2):
            for m in range(PIECES):
                last_copy(m, part).wait_recv()
            integrals(hops, part)
        weights()

    def to_core_late(t, _):
        @pl.when(late)
        def _():
            spots = []
            for u in range(2):
                base = target(2 * t + u) * 4 * rows + side * 2 * rows
                spots.append(pl.ds(pl.multiple_of(base, 2 * rows), 2 * rows))
            lanes = jnp.concatenate([hold[hops, :, spot] for spot in spots], axis=1)
            more = lax.dot_general(
                lanes, weight[...], (((0,), (0,)), ((), ())), preferred_element_type=jnp.float32
            )
            for u in range(2):
                acc[spots[u], :] += more[u * 2 * rows : (u + 1) * 2 * rows, :]

        for u in range(2):
            k = target(2 * t + u)
            core_out[k, side] = acc[chunk(k, side, 1 - core), :].astype(jnp.bfloat16)
            core_copy(k, side, 1).start()
        return 0

    lax.fori_loop(0, n // 2, to_core_late, 0)

    def to_owner(t, _):
        k = target(t)
        cross_copy(k).wait_recv()
        core_copy(k, side, 1).wait_recv()
        mine = acc[chunk(k, side, core), :] + core_in[k, side].astype(jnp.float32)
        mine = (mine + side_in[k].astype(jnp.float32)).astype(jnp.bfloat16)

        @pl.when(t < n - 1)
        def _():
            final[k] = mine
            spread_copy(k, me).start()

        @pl.when(t == n - 1)
        def _():
            out_ref[me] = mine

        return 0

    lax.fori_loop(0, n, to_owner, 0)

    def settle(t, _):
        k = target(t)
        spread_copy(k, k).wait_recv()
        out_ref[k] = land[k]
        return 0

    lax.fori_loop(0, n - 1, settle, 0)

    for slot in range(hops - 1):
        for m in range(PIECES):
            ring_copy(slot, m).wait_send()

    def sent(slot, _):
        @pl.when(jnp.logical_not(handled(slot)))
        def _():
            for m in range(PIECES):
                side_copy(slot, m, side).wait_send()

        return 0

    lax.fori_loop(1, hops, sent, 0)
    for m in range(PIECES):
        last_copy(m, 1 - core).wait_send()

    def closed(t, _):
        k = target(t)
        core_copy(k, 1 - side, 0).wait_send()
        core_copy(k, side, 1).wait_send()
        cross_copy(k).wait_send()

        @pl.when(t < n - 1)
        def _():
            spread_copy(k, me).wait_send()

        return 0

    lax.fori_loop(0, n, closed, 0)


def ring_body(
    factors, occ_level, vir_level, occupied_energy_levels, vir_table, virtual_coefficient_matrix
):
    n = lax.axis_size("occ")
    hops = n // 2
    virt, naux = factors.shape[1], factors.shape[2]
    rows = naux // (n * lax.axis_size("off"))
    smem = pl.BlockSpec(memory_space=pltpu.SMEM)
    vmem = pl.BlockSpec(memory_space=pltpu.VMEM)
    dma = pltpu.SemaphoreType.DMA
    gamma_low = pl.pallas_call(
        functools.partial(pair_kernel, n),
        out_shape=jax.ShapeDtypeStruct((n, rows, virt), jnp.bfloat16),
        in_specs=[
            smem,
            smem,
            pl.BlockSpec(memory_space=pl.ANY),
            vmem,
            vmem,
        ],
        out_specs=vmem,
        scratch_shapes=[
            pltpu.VMEM((1, virt), jnp.float32),
            pltpu.VMEM((virt, 1), jnp.float32),
            pltpu.VMEM((hops + 1, virt, naux), jnp.bfloat16),
            pltpu.VMEM((virt, virt), jnp.float32),
            pltpu.VMEM((virt, virt), jnp.bfloat16),
            pltpu.VMEM((naux, virt), jnp.float32),
            pltpu.VMEM((n, 2, rows, virt), jnp.bfloat16),
            pltpu.VMEM((n, 2, rows, virt), jnp.bfloat16),
            pltpu.VMEM((n, rows, virt), jnp.bfloat16),
            pltpu.VMEM((n, rows, virt), jnp.bfloat16),
            pltpu.VMEM((n, rows, virt), jnp.bfloat16),
            pltpu.VMEM((n, rows, virt), jnp.bfloat16),
            dma,
            dma((hops - 1, PIECES)),
            dma((hops - 1, PIECES)),
            dma((hops - 1, PIECES)),
            dma((hops - 1, PIECES)),
            dma((PIECES,)),
            dma((2 * PIECES,)),
            dma((4, n)),
            dma((2, n)),
            dma((n,)),
            dma((n,)),
        ],
        compiler_params=pltpu.CompilerParams(
            collective_id=0, has_side_effects=True, vmem_limit_bytes=56 * 1024 * 1024
        ),
        cost_estimate=pl.CostEstimate(
            flops=8 * virt * virt * naux, bytes_accessed=2 * virt * naux, transcendentals=0
        ),
    )(occ_level, occupied_energy_levels, factors, vir_level[None, :], vir_table[None, :])
    return jnp.einsum(
        "sbd,dw->sbw",
        gamma_low,
        virtual_coefficient_matrix,
        preferred_element_type=jnp.float32,
    )


def general_body(
    factors, occ_level, vir_level, occupied_energy_levels, vir_table, virtual_coefficient_matrix
):
    off_count = lax.axis_size("off")
    off_index = lax.axis_index("off")
    occ_count = lax.axis_size("occ")
    occ_index = lax.axis_index("occ")
    vir_energy = lookup(vir_level, vir_table)
    occ_energy = lookup(occ_level, occupied_energy_levels)
    own_energy = lax.dynamic_index_in_dim(occ_energy, occ_index, 0, keepdims=False)
    own = factors[0]
    carried = factors
    for bit_pos in range(off_count.bit_length() - 1):
        moved = passed_along(carried, "occ", 1 << bit_pos)
        carried = jnp.where(off_index >> bit_pos & 1 == 1, moved, carried)
    gamma = jnp.zeros((own.shape[1], own.shape[0]), jnp.float32)
    for step_index in range(PAIR_STEPS):
        offset = off_index + off_count * step_index
        pair_companion = (occ_index - offset) % occ_count
        other_energy = lax.dynamic_index_in_dim(occ_energy, pair_companion, 0, keepdims=False)
        other = carried[0]
        if step_index < PAIR_STEPS - 1:
            carried = passed_along(carried, "occ", off_count)
        integral = lax.dot_general(
            own, other, (((1,), (1,)), ((), ())), preferred_element_type=jnp.float32
        )
        denom = vir_energy[:, None] + vir_energy[None, :] - own_energy - other_energy
        amp = integral / denom
        pair_weight = (2.0 * amp - amp.T).astype(jnp.bfloat16)
        gamma = gamma + lax.dot_general(
            other, pair_weight, (((0,), (1,)), ((), ())), preferred_element_type=jnp.float32
        )
    naux_rows = gamma.shape[0]
    per_device = naux_rows // (occ_count * off_count)
    blocks = gamma.reshape(occ_count, off_count, per_device, gamma.shape[1])
    total = lax.psum(blocks, "off")
    mine = lax.dynamic_slice_in_dim(total, off_index, 1, 1)
    lower_gamma_part = mine.reshape(occ_count, per_device, gamma.shape[1]).astype(jnp.bfloat16)
    finished_flag = jnp.einsum(
        "sbd,dw->sbw",
        lower_gamma_part,
        virtual_coefficient_matrix,
        preferred_element_type=jnp.float32,
    )
    moved_back = lax.all_to_all(finished_flag[None], "occ", split_axis=1, concat_axis=0, tiled=True)
    return moved_back.reshape(moved_back.shape[0], per_device, virtual_coefficient_matrix.shape[1])


def solution(mesh):
    in_specs = (P("occ", None, None), P(), P(), P(), P(), P())
    out_specs = P(None, ("occ", "off"), None)
    every_pair = mesh.shape["occ"] == mesh.shape["off"] * PAIR_STEPS
    ring = every_pair and mesh.shape["off"] == 4
    body = ring_body if ring else general_body
    return jax.shard_map(body, mesh=mesh, in_specs=in_specs, out_specs=out_specs, check_vma=False)
```

```python
import functools

import jax
import jax.numpy as jnp
from jax import lax
from jax.experimental import pallas as pl
from jax.experimental.pallas import tpu as pltpu
from jax.sharding import PartitionSpec as P

PAIR_STEPS = 2
PIECES = 4
MESH = pl.DeviceIdType.MESH


def passed_along(value, axis, by):
    length = lax.axis_size(axis)
    return lax.ppermute(value, axis, [(i, (i + by) % length) for i in range(length)])


def lookup(level, table):
    hits = level[:, None] == jnp.arange(table.shape[0], dtype=jnp.int32)[None, :]
    return jnp.sum(jnp.where(hits, table[None, :], jnp.float32(0.0)), axis=1)


def ring_place(occ, n):
    return jnp.where(occ % 2 == 0, occ // 2, n - 1 - occ // 2)


def ring_member(place, n):
    return jnp.where(place < n // 2, 2 * place, 2 * (n - 1 - place) + 1)


def pair_kernel(
    n,
    occ_level_ref,
    occ_table_ref,
    factors_ref,
    vir_level_ref,
    vir_table_ref,
    out_ref,
    ev_row_ref,
    ev_col_ref,
    hold,
    amp,
    weight,
    acc,
    core_out,
    core_in,
    side_out,
    side_in,
    final,
    land,
    load_sem,
    ring_send,
    ring_recv,
    side_send,
    side_recv,
    last_send,
    last_recv,
    core_sems,
    cross_sems,
    spread_send,
    spread_recv,
):
    hops = n // 2
    virt, naux = hold.shape[1], hold.shape[2]
    half = virt // 2
    piece = half // PIECES
    rows = land.shape[1]
    me = lax.axis_index("occ")
    off = lax.axis_index("off")
    side, core = off // 2, off % 2
    place = ring_place(me, n)
    up = ring_member(lax.rem(place + 1, n), n)
    down = ring_member(lax.rem(place + n - 1, n), n)
    onward = jnp.where(core == 0, up, down)
    other_side = (1 - side) * 2 + core
    other_core = side * 2 + (1 - core)

    load = pltpu.make_async_copy(factors_ref.at[0], hold.at[0], load_sem)
    load.start()

    barrier = pltpu.get_barrier_semaphore()
    for step in range(1, n):
        pl.semaphore_signal(
            barrier, inc=1, device_id=(lax.rem(me + step, n), off), device_id_type=MESH
        )
    for step in range(1, 4):
        peer = lax.rem(off + step, 4)
        for node in (me, up, down):
            pl.semaphore_signal(barrier, inc=1, device_id=(node, peer), device_id_type=MESH)
    pl.semaphore_wait(barrier, n - 1 + 9)

    def ring_copy(slot, m, source=None):
        where = pl.ds(pl.multiple_of(side * half + m * piece, piece), piece)
        return pltpu.make_async_remote_copy(
            src_ref=hold.at[slot, where] if source is None else source.at[0, where],
            dst_ref=hold.at[slot + 1, where],
            send_sem=ring_send.at[slot, m],
            recv_sem=ring_recv.at[slot, m],
            device_id=(onward, off),
            device_id_type=MESH,
        )

    def side_copy(slot, m, from_side):
        where = pl.ds(pl.multiple_of(from_side * half + m * piece, piece), piece)
        return pltpu.make_async_remote_copy(
            src_ref=hold.at[slot, where],
            dst_ref=hold.at[slot, where],
            send_sem=side_send.at[slot - 1, m],
            recv_sem=side_recv.at[slot - 1, m],
            device_id=(me, other_side),
            device_id_type=MESH,
        )

    def last_copy(m, part):
        where = pl.ds(pl.multiple_of(part * half + m * piece, piece), piece)
        return pltpu.make_async_remote_copy(
            src_ref=hold.at[hops - 1, where],
            dst_ref=hold.at[hops, where],
            send_sem=last_send.at[m],
            recv_sem=last_recv.at[part * PIECES + m],
            device_id=(onward, side * 2 + (1 - side)),
            device_id_type=MESH,
        )

    def handled(slot):
        turn = lax.rem(slot + side + core, 2) == 1
        return jnp.logical_and(turn, jnp.logical_or(core == 0, slot > 0))

    def occ_energy(orbital):
        return occ_table_ref[occ_level_ref[orbital]]

    def integrals(slot, h):
        turn = jnp.where(core == 0, n - slot, slot)
        partner = ring_member(lax.rem(place + turn, n), n)
        pair_energy = occ_energy(me) + occ_energy(partner)
        at = pl.ds(pl.multiple_of(h * half, half), half)
        integral = lax.dot_general(
            hold[slot, at, :],
            hold[0],
            (((1,), (1,)), ((), ())),
            preferred_element_type=jnp.float32,
        )
        amp[at, :] = integral / (ev_col_ref[at, :] + ev_row_ref[...] - pair_energy)

    def weights():
        third = virt // 3
        for b in range(3):
            for a in range(3):
                bs, as_ = pl.ds(b * third, third), pl.ds(a * third, third)
                weight[bs, as_] = (2.0 * amp[bs, as_] - amp[as_, bs].T).astype(jnp.bfloat16)

    def gammas(slot, p, part):
        at = pl.ds(pl.multiple_of(p * part, part), part)
        acc[at, :] += lax.dot_general(
            hold[slot, :, at],
            weight[...],
            (((0,), (0,)), ((), ())),
            preferred_element_type=jnp.float32,
        )

    def work(slot, m):
        if m == 0:
            integrals(slot, side)
        elif m == 1:

            @pl.when(jnp.logical_and(slot > 0, slot < hops - 1))
            def _():
                for q in range(PIECES):
                    side_copy(slot, q, 1 - side).wait_recv()

            integrals(slot, 1 - side)
        else:
            if m == 2:
                weights()

            def two(p, _):
                gammas(slot, 2 * (m - 2) + p, naux // 4)
                return 0

            lax.fori_loop(0, 2, two, 0)

    for m in range(PIECES):
        ring_copy(0, m, factors_ref).start()

    def clear(p, _):
        at = pl.ds(pl.multiple_of(p * 4 * rows, 4 * rows), 4 * rows)
        acc[at, :] = jnp.zeros((4 * rows, virt), jnp.float32)
        return 0

    lax.fori_loop(0, n, clear, 0)
    load.wait()

    levels = vir_table_ref.shape[0]
    same = lax.broadcasted_iota(jnp.int32, (levels, levels), 0) == lax.broadcasted_iota(
        jnp.int32, (levels, levels), 1
    )
    table = jnp.sum(jnp.where(same, vir_table_ref[...].reshape(1, levels), 0.0), axis=1, keepdims=True)
    hits = lax.broadcasted_iota(jnp.int32, (levels, virt), 0) == vir_level_ref[...].reshape(1, virt)
    row = jnp.sum(jnp.where(hits, table, 0.0), axis=0, keepdims=True)
    ev_row_ref[...] = row
    same = lax.broadcasted_iota(jnp.int32, (virt, virt), 0) == lax.broadcasted_iota(
        jnp.int32, (virt, virt), 1
    )
    ev_col_ref[...] = jnp.sum(jnp.where(same, row, 0.0), axis=1, keepdims=True)

    def stage(slot, _):
        for m in range(PIECES):

            @pl.when(slot < hops)
            def _():
                ring_copy(slot - 1, m).wait_recv()

                @pl.when(slot < hops - 1)
                def _():
                    ring_copy(slot, m).start()

                @pl.when(jnp.logical_not(handled(slot)))
                def _():
                    side_copy(slot, m, side).start()

            @pl.when(jnp.logical_and(slot == hops - 1, jnp.logical_not(handled(slot))))
            def _():
                last_copy(m, 1 - core).start()

            if m == 0:

                @pl.when(jnp.logical_and(slot == hops, handled(hops - 1)))
                def _():
                    for q in range(PIECES):
                        side_copy(hops - 1, q, 1 - side).wait_recv()
                        last_copy(q, 1 - core).start()

            @pl.when(handled(slot - 1))
            def _():
                work(slot - 1, m)

        return 0

    lax.fori_loop(1, hops + 1, stage, 0)

    late = handled(hops)

    def core_copy(k, s, when):
        return pltpu.make_async_remote_copy(
            src_ref=core_out.at[k, s],
            dst_ref=core_in.at[k, s],
            send_sem=core_sems.at[2 * when, k],
            recv_sem=core_sems.at[2 * when + 1, k],
            device_id=(me, other_core),
            device_id_type=MESH,
        )

    def cross_copy(k):
        return pltpu.make_async_remote_copy(
            src_ref=side_out.at[k],
            dst_ref=side_in.at[k],
            send_sem=cross_sems.at[0, k],
            recv_sem=cross_sems.at[1, k],
            device_id=(me, other_side),
            device_id_type=MESH,
        )

    def spread_copy(k, source):
        return pltpu.make_async_remote_copy(
            src_ref=final.at[k],
            dst_ref=land.at[source],
            send_sem=spread_send.at[k],
            recv_sem=spread_recv.at[source],
            device_id=(k, off),
            device_id_type=MESH,
        )

    def chunk(k, s, c):
        return pl.ds(pl.multiple_of(((k * 2 + s) * 2 + c) * rows, rows), rows)

    def target(t):
        flip = jnp.where(t < n // 2, n // 2 + t, n - 1 - t)
        k = 0
        for bit in range(n.bit_length() - 1):
            k = k + ((me // 2**bit + flip // 2**bit) % 2) * 2**bit
        return k

    def to_core(t, _):
        k = target(t)
        core_out[k, 1 - side] = acc[chunk(k, 1 - side, 1 - core), :].astype(jnp.bfloat16)
        core_copy(k, 1 - side, 0).start()
        return 0

    lax.fori_loop(0, n, to_core, 0)

    def to_side(t, _):
        k = target(t)
        core_copy(k, 1 - side, 0).wait_recv()
        theirs = acc[chunk(k, 1 - side, core), :] + core_in[k, 1 - side].astype(jnp.float32)
        side_out[k] = theirs.astype(jnp.bfloat16)
        cross_copy(k).start()
        return 0

    lax.fori_loop(0, n, to_side, 0)

    @pl.when(late)
    def _():
        for part in (side, 1 - side):
            for m in range(PIECES):
                last_copy(m, part).wait_recv()
            integrals(hops, part)
        weights()

    def to_core_late(t, _):
        @pl.when(late)
        def _():
            spots = []
            for u in range(2):
                base = target(2 * t + u) * 4 * rows + side * 2 * rows
                spots.append(pl.ds(pl.multiple_of(base, 2 * rows), 2 * rows))
            lanes = jnp.concatenate([hold[hops, :, spot] for spot in spots], axis=1)
            more = lax.dot_general(
                lanes, weight[...], (((0,), (0,)), ((), ())), preferred_element_type=jnp.float32
            )
            for u in range(2):
                acc[spots[u], :] += more[u * 2 * rows : (u + 1) * 2 * rows, :]

        for u in range(2):
            k = target(2 * t + u)
            core_out[k, side] = acc[chunk(k, side, 1 - core), :].astype(jnp.bfloat16)
            core_copy(k, side, 1).start()
        return 0

    def to_owner(t, _):
        k = target(t)
        cross_copy(k).wait_recv()
        core_copy(k, side, 1).wait_recv()
        mine = acc[chunk(k, side, core), :] + core_in[k, side].astype(jnp.float32)
        mine = (mine + side_in[k].astype(jnp.float32)).astype(jnp.bfloat16)

        @pl.when(t < n - 1)
        def _():
            final[k] = mine
            spread_copy(k, me).start()

        @pl.when(t == n - 1)
        def _():
            out_ref[me] = mine

        return 0

    def finish(t, _):
        to_core_late(t, 0)
        for u in range(2):
            to_owner(2 * t + u, 0)
        return 0

    lax.fori_loop(0, n // 2, finish, 0)

    def settle(t, _):
        k = target(t)
        spread_copy(k, k).wait_recv()
        out_ref[k] = land[k]
        return 0

    lax.fori_loop(0, n - 1, settle, 0)

    for slot in range(hops - 1):
        for m in range(PIECES):
            ring_copy(slot, m, factors_ref if slot == 0 else None).wait_send()

    def sent(slot, _):
        @pl.when(jnp.logical_not(handled(slot)))
        def _():
            for m in range(PIECES):
                side_copy(slot, m, side).wait_send()

        return 0

    lax.fori_loop(1, hops, sent, 0)
    for m in range(PIECES):
        last_copy(m, 1 - core).wait_send()

    def closed(t, _):
        k = target(t)
        core_copy(k, 1 - side, 0).wait_send()
        core_copy(k, side, 1).wait_send()
        cross_copy(k).wait_send()

        @pl.when(t < n - 1)
        def _():
            spread_copy(k, me).wait_send()

        return 0

    lax.fori_loop(0, n, closed, 0)


def ring_body(
    factors, occ_level, vir_level, occupied_energy_levels, vir_table, virtual_coefficient_matrix
):
    n = lax.axis_size("occ")
    hops = n // 2
    virt, naux = factors.shape[1], factors.shape[2]
    rows = naux // (n * lax.axis_size("off"))
    smem = pl.BlockSpec(memory_space=pltpu.SMEM)
    vmem = pl.BlockSpec(memory_space=pltpu.VMEM)
    dma = pltpu.SemaphoreType.DMA
    gamma_low = pl.pallas_call(
        functools.partial(pair_kernel, n),
        out_shape=jax.ShapeDtypeStruct((n, rows, virt), jnp.bfloat16),
        in_specs=[
            smem,
            smem,
            pl.BlockSpec(memory_space=pl.ANY),
            vmem,
            vmem,
        ],
        out_specs=vmem,
        scratch_shapes=[
            pltpu.VMEM((1, virt), jnp.float32),
            pltpu.VMEM((virt, 1), jnp.float32),
            pltpu.VMEM((hops + 1, virt, naux), jnp.bfloat16),
            pltpu.VMEM((virt, virt), jnp.float32),
            pltpu.VMEM((virt, virt), jnp.bfloat16),
            pltpu.VMEM((naux, virt), jnp.float32),
            pltpu.VMEM((n, 2, rows, virt), jnp.bfloat16),
            pltpu.VMEM((n, 2, rows, virt), jnp.bfloat16),
            pltpu.VMEM((n, rows, virt), jnp.bfloat16),
            pltpu.VMEM((n, rows, virt), jnp.bfloat16),
            pltpu.VMEM((n, rows, virt), jnp.bfloat16),
            pltpu.VMEM((n, rows, virt), jnp.bfloat16),
            dma,
            dma((hops - 1, PIECES)),
            dma((hops - 1, PIECES)),
            dma((hops - 1, PIECES)),
            dma((hops - 1, PIECES)),
            dma((PIECES,)),
            dma((2 * PIECES,)),
            dma((4, n)),
            dma((2, n)),
            dma((n,)),
            dma((n,)),
        ],
        compiler_params=pltpu.CompilerParams(
            collective_id=0, has_side_effects=True, vmem_limit_bytes=56 * 1024 * 1024
        ),
        cost_estimate=pl.CostEstimate(
            flops=8 * virt * virt * naux, bytes_accessed=2 * virt * naux, transcendentals=0
        ),
    )(occ_level, occupied_energy_levels, factors, vir_level, vir_table)
    return jnp.einsum(
        "sbd,dw->sbw",
        gamma_low,
        virtual_coefficient_matrix,
        preferred_element_type=jnp.float32,
    )


def general_body(
    factors, occ_level, vir_level, occupied_energy_levels, vir_table, virtual_coefficient_matrix
):
    off_count = lax.axis_size("off")
    off_index = lax.axis_index("off")
    occ_count = lax.axis_size("occ")
    occ_index = lax.axis_index("occ")
    vir_energy = lookup(vir_level, vir_table)
    occ_energy = lookup(occ_level, occupied_energy_levels)
    own_energy = lax.dynamic_index_in_dim(occ_energy, occ_index, 0, keepdims=False)
    own = factors[0]
    carried = factors
    for bit_pos in range(off_count.bit_length() - 1):
        moved = passed_along(carried, "occ", 1 << bit_pos)
        carried = jnp.where(off_index >> bit_pos & 1 == 1, moved, carried)
    gamma = jnp.zeros((own.shape[1], own.shape[0]), jnp.float32)
    for step_index in range(PAIR_STEPS):
        offset = off_index + off_count * step_index
        pair_companion = (occ_index - offset) % occ_count
        other_energy = lax.dynamic_index_in_dim(occ_energy, pair_companion, 0, keepdims=False)
        other = carried[0]
        if step_index < PAIR_STEPS - 1:
            carried = passed_along(carried, "occ", off_count)
        integral = lax.dot_general(
            own, other, (((1,), (1,)), ((), ())), preferred_element_type=jnp.float32
        )
        denom = vir_energy[:, None] + vir_energy[None, :] - own_energy - other_energy
        amp = integral / denom
        pair_weight = (2.0 * amp - amp.T).astype(jnp.bfloat16)
        gamma = gamma + lax.dot_general(
            other, pair_weight, (((0,), (1,)), ((), ())), preferred_element_type=jnp.float32
        )
    naux_rows = gamma.shape[0]
    per_device = naux_rows // (occ_count * off_count)
    blocks = gamma.reshape(occ_count, off_count, per_device, gamma.shape[1])
    total = lax.psum(blocks, "off")
    mine = lax.dynamic_slice_in_dim(total, off_index, 1, 1)
    lower_gamma_part = mine.reshape(occ_count, per_device, gamma.shape[1]).astype(jnp.bfloat16)
    finished_flag = jnp.einsum(
        "sbd,dw->sbw",
        lower_gamma_part,
        virtual_coefficient_matrix,
        preferred_element_type=jnp.float32,
    )
    moved_back = lax.all_to_all(finished_flag[None], "occ", split_axis=1, concat_axis=0, tiled=True)
    return moved_back.reshape(moved_back.shape[0], per_device, virtual_coefficient_matrix.shape[1])


def solution(mesh):
    in_specs = (P("occ", None, None), P(), P(), P(), P(), P())
    out_specs = P(None, ("occ", "off"), None)
    every_pair = mesh.shape["occ"] == mesh.shape["off"] * PAIR_STEPS
    ring = every_pair and mesh.shape["off"] == 4
    body = ring_body if ring else general_body
    return jax.shard_map(body, mesh=mesh, in_specs=in_specs, out_specs=out_specs, check_vma=False)
```
